32 devices in a mesh: seq: 8 (over z, y), head: 4 (over x, core).
Axes of the slice: x: 2, y: 2, z: 4, core: 2. Of those that a mesh axis runs over, the one named last changes fastest.
Arguments:
- query_proj: bfloat16 [2048, 2048], P('seq', 'head'), may hold values from -40 to 40
- key_proj: bfloat16 [2048, 2048], P('seq', 'head'), may hold values from -40 to 40
- value_proj: bfloat16 [2048, 4096], P('seq', 'head'), may hold values from -40 to 40
- gate_proj: bfloat16 [2048, 4096], P('seq', 'head'), may hold values from -6 to 6
- strength: float32 [32, 2048], P('head', 'seq'), may hold values from 0 to 2, as said below
- log_decay: float32 [32, 2048], P('head', 'seq'), may hold values from -1 to 0, as said below
- conv_query: bfloat16 [4, 2048], P(None, 'head'), may hold values from -3 to 3
- conv_key: bfloat16 [4, 2048], P(None, 'head'), may hold values from -3 to 3
- conv_value: bfloat16 [4, 4096], P(None, 'head'), may hold values from -3 to 3
- norm_gain: bfloat16 [128], replicated, may hold values from 0.099609375 to 1.8984375
- out_weight: bfloat16 [4096, 2048], P('head'), may hold values from -0.09375 to 0.09375
Outputs:
- layer_out: bfloat16 [2048, 2048], P(('seq', 'head'))
The draws below stay inside these ranges and needn't reach their ends.
Inputs may be any that keep to these rules, and one draw needn't show every extreme that they name: `strength`: strictly inside the range. `log_decay`: strictly below the upper end.
All inputs are finite; a program needn't handle non-finite values.
Results may differ from the reference program's by a relative error of at most 0.014.
Values may be sent and summed in bfloat16 or wider, within the bound.
A program may use at most 64 MiB of HBM per device.

```python
import math
import jax
import jax.numpy as jnp
from jax import lax

D = 2048
HK = 16
HV = 32
DK = 128
DV = 128
KCONV = 4
SPAN = 128
TOK_DEV = 256
SEQUENCE_TOKENS = 2048
N_HEAD = 4


def slow_heads(key):
    head_kinds = jax.random.randint(jax.random.fold_in(key, 101), (HV,), 0, 8)
    fast_cut = 4
    return head_kinds >= fast_cut


def rough_field(key, row_count, col_count, col_spread, early_gain):
    key_base = jax.random.fold_in(key, 1)
    key_rows = jax.random.fold_in(key, 2)
    key_cols = jax.random.fold_in(key, 3)
    base_values = jax.random.truncated_normal(key_base, -4.0, 4.0, (row_count, col_count), jnp.float32)
    row_scale = jnp.exp(jax.random.uniform(key_rows, (row_count, 1), jnp.float32, -1.1, 1.1))
    col_scale = jnp.exp(jax.random.uniform(key_cols, (1, col_count), jnp.float32, -col_spread, col_spread))
    row_index = jnp.arange(row_count)
    early_rows = jnp.where(row_index < row_count // 8, early_gain, 1.0)[:, None]
    return jnp.clip(base_values * row_scale * col_scale * early_rows, -40.0, 40.0)


def draw_query_proj(key, part):
    return rough_field(jax.random.fold_in(key, 21), SEQUENCE_TOKENS, HK * DK, 1.1, 1.0).astype(jnp.bfloat16)


def draw_key_proj(key, part):
    return rough_field(jax.random.fold_in(key, 22), SEQUENCE_TOKENS, HK * DK, 1.4, 1.0).astype(jnp.bfloat16)


def draw_value_proj(key, part):
    return rough_field(jax.random.fold_in(key, 23), SEQUENCE_TOKENS, HV * DV, 1.1, 3.0).astype(jnp.bfloat16)


def draw_strength(key, part):
    slow_mask = slow_heads(key)
    key_level = jax.random.fold_in(key, 31)
    key_jitter = jax.random.fold_in(key, 32)
    key_fast = jax.random.fold_in(key, 33)
    level_low, level_high, fast_low, fast_high = (1.5, 6.0, 0.2, 1.8)
    head_level = jnp.exp(jax.random.uniform(key_level, (HV, 1), jnp.float32, math.log(level_low), math.log(level_high))) * (DK / SEQUENCE_TOKENS)
    jitter = jax.random.uniform(key_jitter, (HV, SEQUENCE_TOKENS), jnp.float32, 0.5, 1.5)
    fast_values = jax.random.uniform(key_fast, (HV, SEQUENCE_TOKENS), jnp.float32, fast_low, fast_high)
    return jnp.where(slow_mask[:, None], jnp.minimum(head_level * jitter, 1.9), fast_values)


def draw_log_decay(key, part):
    slow_mask = slow_heads(key)
    key_fast = jax.random.fold_in(key, 41)
    key_slow = jax.random.fold_in(key, 42)
    key_block = jax.random.fold_in(key, 43)
    key_jitter = jax.random.fold_in(key, 44)
    key_locations = jax.random.fold_in(key, 45)
    key_depth = jax.random.fold_in(key, 46)
    fast_rate = jnp.exp(jax.random.uniform(key_fast, (HV, 1), jnp.float32, math.log(1.0 / 50.0), math.log(1.0 / 30.0)))
    slow_rate = jnp.exp(jax.random.uniform(key_slow, (HV, 1), jnp.float32, math.log(0.2), math.log(0.6))) / SEQUENCE_TOKENS
    blocks = SEQUENCE_TOKENS // TOK_DEV
    block_factor = jnp.exp(jax.random.uniform(key_block, (HV, blocks, 1), jnp.float32, math.log(0.5), math.log(2.0)))
    block_factor = jnp.broadcast_to(block_factor, (HV, blocks, TOK_DEV)).reshape(HV, SEQUENCE_TOKENS)
    jitter = jax.random.uniform(key_jitter, (HV, SEQUENCE_TOKENS), jnp.float32, 0.5, 1.5)
    decay_speed = jnp.where(slow_mask[:, None], slow_rate, fast_rate) * block_factor * jitter
    spike_locations = jax.random.randint(key_locations, (2,), 0, SEQUENCE_TOKENS)
    layer_depths = jax.random.uniform(key_depth, (HV, 2), jnp.float32, math.log(0.5), math.log(0.8))
    column_index = jnp.arange(SEQUENCE_TOKENS)
    spike_events = jnp.where(column_index[None, :] == spike_locations[0], layer_depths[:, 0:1], 0.0)
    spike_events = spike_events + jnp.where(column_index[None, :] == spike_locations[1], layer_depths[:, 1:2], 0.0)
    return spike_events - decay_speed


def level_of(key, extent, pieces, smallest, largest):
    def one(dim, shards_of):
        draws = jax.random.uniform(jax.random.fold_in(jax.random.fold_in(key, 6), dim), (shards_of,), jnp.float32, smallest / len(pieces), largest / len(pieces))
        return jnp.repeat(jnp.exp(draws), extent[dim] // shards_of).reshape((-1,) + (1,) * (len(extent) - dim - 1))

    loudness = one(*pieces[0])
    for cut in pieces[1:]:
        loudness = loudness * one(*cut)
    return loudness


def normal_values(rng, extent, scale, most, shards=(), held_as=jnp.bfloat16):
    entries = scale * jax.random.normal(rng, extent, jnp.float32)
    if shards:
        entries = entries * level_of(rng, extent, shards, -0.22, 0.18)
    return jnp.clip(entries, -most, most).astype(held_as)


def setup_inputs(seed: int = 0) -> dict:
    key_list = jax.random.split(jax.random.key(seed), 12)
    query_proj = draw_query_proj(jax.random.fold_in(key_list[11], 71), 0)
    key_proj = draw_key_proj(jax.random.fold_in(key_list[11], 71), 0)
    value_proj = draw_value_proj(jax.random.fold_in(key_list[11], 71), 0)
    gate_proj = normal_values(key_list[3], (SEQUENCE_TOKENS, HV * DV), 1.0, 6.0, ((0, 8), (1, 4)))
    strength = draw_strength(jax.random.fold_in(key_list[11], 71), 0)
    log_decay = draw_log_decay(jax.random.fold_in(key_list[11], 71), 0)
    conv_query = normal_values(key_list[6], (KCONV, HK * DK), KCONV ** -0.5, 3.0, ((1, 4),))
    conv_key = normal_values(key_list[7], (KCONV, HK * DK), KCONV ** -0.5, 3.0, ((1, 4),))
    conv_value = normal_values(key_list[8], (KCONV, HV * DV), KCONV ** -0.5, 3.0, ((1, 4),))
    norm_gain = jnp.clip(1.0 + 0.18 * jax.random.normal(key_list[9], (DV,), jnp.float32), 0.099609375, 1.8984375).astype(jnp.bfloat16)
    out_weight = normal_values(key_list[10], (HV * DV, D), (HV * DV) ** -0.5, 0.09375, ((0, 4),))
    return dict(query_proj=query_proj, key_proj=key_proj, value_proj=value_proj, gate_proj=gate_proj, strength=strength, log_decay=log_decay, conv_query=conv_query, conv_key=conv_key, conv_value=conv_value, norm_gain=norm_gain, out_weight=out_weight)


epsilon = 1e-06
highest = lax.Precision.HIGHEST

def conv_silu(signal, weights):
    length = signal.shape[0]
    padded = jnp.concatenate([jnp.zeros((KCONV - 1, signal.shape[1]), jnp.float32), signal.astype(jnp.float32)], axis=0)
    conv_taps = weights.astype(jnp.float32)
    summed = jnp.zeros((length, signal.shape[1]), jnp.float32)
    for offset in range(KCONV):
        summed = summed + conv_taps[offset] * padded[offset:offset + length]
    return jax.nn.silu(summed)

def advance(state_now, span_in):
    query_span, key_span, value_span, strength_span, decay_span = span_in
    cumulative = jnp.cumsum(decay_span, axis=-1)
    positions = jnp.arange(SPAN)
    inclusive = positions[:, None] >= positions[None, :]
    strictly = positions[:, None] > positions[None, :]
    log_gaps = cumulative[:, :, None] - cumulative[:, None, :]
    decays = jnp.where(inclusive, jnp.exp(jnp.where(inclusive, log_gaps, 0.0)), 0.0)
    key_key = jnp.dot(key_span, key_span.T, precision=highest)
    query_key = jnp.dot(query_span, key_span.T, precision=highest)
    lower_part = jnp.where(strictly, strength_span[:, :, None] * decays * key_key[None], 0.0)
    system = lower_part + jnp.eye(SPAN, dtype=jnp.float32)
    right_side = jnp.concatenate([strength_span[:, :, None] * value_span, (strength_span * jnp.exp(cumulative))[:, :, None] * key_span[None]], axis=-1)
    solved = lax.linalg.triangular_solve(system, right_side, left_side=True, lower=True, unit_diagonal=True)
    written = solved[..., :DV] - jnp.einsum('rck,rkv->rcv', solved[..., DV:], state_now, precision=highest)
    attention = decays * query_key[None]
    outputs = jnp.einsum('rck,rkv->rcv', jnp.exp(cumulative)[:, :, None] * query_span[None], state_now, precision=highest)
    outputs = outputs + jnp.einsum('rce,rev->rcv', attention, written, precision=highest)
    span_end = cumulative[:, -1:]
    scaled_keys = jnp.exp(span_end - cumulative)[:, :, None] * key_span[None]
    state_next = jnp.exp(span_end)[:, :, None] * state_now + jnp.einsum('rck,rcv->rkv', scaled_keys, written, precision=highest)
    return (state_next, outputs)

def reference(query_proj, key_proj, value_proj, gate_proj, strength, log_decay, conv_query, conv_key, conv_value, norm_gain, out_weight):
    ratio_heads = HV // HK
    group_width = ratio_heads * DV
    spans = SEQUENCE_TOKENS // SPAN
    gain_values = norm_gain.astype(jnp.float32)

    def head_core(packed):
        query_raw, key_raw, value_raw, gate_raw, strength_head, decay_head, query_taps, key_taps, value_taps = packed
        queries = conv_silu(query_raw, query_taps)
        key_rows = conv_silu(key_raw, key_taps)
        key_rows = key_rows / jnp.sqrt(lax.optimization_barrier(jnp.sum(key_rows * key_rows, axis=-1, keepdims=True)) + epsilon)
        values = conv_silu(value_raw, value_taps)
        query_blocks = queries.reshape(spans, SPAN, DK)
        key_blocks = key_rows.reshape(spans, SPAN, DK)
        value_blocks = values.reshape(spans, SPAN, ratio_heads, DV).transpose(0, 2, 1, 3)
        strength_blocks = strength_head.reshape(ratio_heads, spans, SPAN).transpose(1, 0, 2)
        decay_blocks = decay_head.reshape(ratio_heads, spans, SPAN).transpose(1, 0, 2)
        zero_state = jnp.zeros((ratio_heads, DK, DV), jnp.float32)
        ignored, outputs = lax.scan(advance, zero_state, (query_blocks, key_blocks, value_blocks, strength_blocks, decay_blocks))
        core_out = outputs.transpose(0, 2, 1, 3).reshape(SEQUENCE_TOKENS, ratio_heads, DV)
        gate_values = gate_raw.astype(jnp.float32).reshape(SEQUENCE_TOKENS, ratio_heads, DV)
        scale_rows = lax.rsqrt(lax.optimization_barrier(jnp.mean(core_out * core_out, axis=-1, keepdims=True)) + epsilon)
        normed = core_out * scale_rows * gain_values * jax.nn.silu(gate_values)
        return normed.reshape(SEQUENCE_TOKENS, group_width).astype(jnp.bfloat16)
    query_stack = query_proj.reshape(SEQUENCE_TOKENS, HK, DK).transpose(1, 0, 2)
    key_stack = key_proj.reshape(SEQUENCE_TOKENS, HK, DK).transpose(1, 0, 2)
    value_stack = value_proj.reshape(SEQUENCE_TOKENS, HK, group_width).transpose(1, 0, 2)
    gate_stack = gate_proj.reshape(SEQUENCE_TOKENS, HK, group_width).transpose(1, 0, 2)
    strength_stack = strength.reshape(HK, ratio_heads, SEQUENCE_TOKENS)
    decay_stack = log_decay.reshape(HK, ratio_heads, SEQUENCE_TOKENS)
    query_taps = conv_query.reshape(KCONV, HK, DK).transpose(1, 0, 2)
    key_taps = conv_key.reshape(KCONV, HK, DK).transpose(1, 0, 2)
    value_taps = conv_value.reshape(KCONV, HK, group_width).transpose(1, 0, 2)
    hidden = lax.map(head_core, (query_stack, key_stack, value_stack, gate_stack, strength_stack, decay_stack, query_taps, key_taps, value_taps))
    hidden = hidden.transpose(1, 0, 2).reshape(SEQUENCE_TOKENS, HV * DV)
    group_cols = HV * DV // N_HEAD
    summed = jnp.zeros((SEQUENCE_TOKENS, D), jnp.float32)
    for group in range(N_HEAD):
        lower_col = group * group_cols
        partial_sum = jnp.dot(hidden[:, lower_col:lower_col + group_cols].astype(jnp.float32), out_weight[lower_col:lower_col + group_cols].astype(jnp.float32), preferred_element_type=jnp.float32).astype(jnp.bfloat16)
        summed = summed + lax.optimization_barrier(partial_sum).astype(jnp.float32)
    return summed.astype(jnp.bfloat16)
```

```python
import functools

import jax
import jax.numpy as jnp
from jax import lax
from jax.experimental import pallas as pl
from jax.experimental.pallas import tpu as pltpu
from jax.sharding import PartitionSpec as P

DK = 128
HALF = 128
RIM = 16
EPSILON = 1e-06
MESH = pl.DeviceIdType.MESH
f32 = jnp.float32
bf16 = jnp.bfloat16
STATE = f32
CHUNK = 512


def dot(a, b):
    return jnp.dot(a.astype(bf16), b.astype(bf16), preferred_element_type=f32)


def dot_nt(a, b, precision=None):
    return lax.dot_general(
        a, b, (((1,), (1,)), ((), ())), precision=precision, preferred_element_type=f32
    )


def dot_tn(a, b):
    return lax.dot_general(
        a.astype(bf16), b.astype(bf16), (((0,), (0,)), ((), ())), preferred_element_type=f32
    )


def silu(x):
    return x / (1.0 + jnp.exp(-x))


def lower_inverses(systems, masks_ref):
    size = systems[0].shape[0]
    row = lax.broadcasted_iota(jnp.int32, (size, size), 0)
    col = lax.broadcasted_iota(jnp.int32, (size, size), 1)
    eye = (row == col).astype(f32)
    lows = [low.astype(bf16) for low in systems]
    inverses = [eye - (low * masks_ref[0]).astype(f32) for low in lows]
    for level in range(1, masks_ref.shape[0]):
        held = [inverse.astype(bf16) for inverse in inverses]
        inner = [dot(low * masks_ref[level], x) for low, x in zip(lows, held)]
        inverses = [old - dot(x, y) for old, x, y in zip(inverses, held, inner)]
    return inverses


def kernel(
    seq_count,
    head_count,
    q_ref,
    k_ref,
    v_ref,
    g_ref,
    beta_ref,
    decay_ref,
    cq_ref,
    ck_ref,
    cv_ref,
    gain_ref,
    w_hbm,
    out_ref,
    rim_q,
    rim_k,
    rim_v,
    conv_s,
    masks_s,
    ccol_s,
    bcol_s,
    crow_s,
    inject_s,
    transit_s,
    end_s,
    local_s,
    couple_s,
    send_s,
    recv_s,
    hidden_s,
    w_s,
    part_s,
    gather_s,
    w_sem,
    rim_send,
    rim_recv,
    state_send,
    state_recv,
    part_send,
    part_recv,
):
    me = lax.axis_index("seq")
    mine = lax.axis_index("head")
    length, key_cols = q_ref.shape
    key_heads = key_cols // DK
    value_heads = v_ref.shape[1] // DK
    ratio = value_heads // key_heads
    has_before = me > 0
    has_after = me < seq_count - 1
    after = lax.rem(me + 1, seq_count)
    before = lax.rem(me + seq_count - 1, seq_count)

    w_copy = pltpu.make_async_copy(w_hbm, w_s, w_sem)
    w_copy.start()

    barrier = pltpu.get_barrier_semaphore()

    @pl.when(has_before)
    def _():
        pl.semaphore_signal(barrier, inc=1, device_id={"seq": before}, device_id_type=MESH)

    @pl.when(has_after)
    def _():
        pl.semaphore_signal(barrier, inc=1, device_id={"seq": after}, device_id_type=MESH)

    for step in range(1, head_count):
        pl.semaphore_signal(
            barrier,
            inc=1,
            device_id={"head": lax.rem(mine + step, head_count)},
            device_id_type=MESH,
        )
    pl.semaphore_wait(
        barrier, head_count - 1 + has_before.astype(jnp.int32) + has_after.astype(jnp.int32)
    )

    def rim_copies():
        return [
            pltpu.make_async_remote_copy(
                src_ref=source.at[pl.ds(length - RIM, RIM)],
                dst_ref=target,
                send_sem=rim_send.at[slot],
                recv_sem=rim_recv.at[slot],
                device_id={"seq": after},
                device_id_type=MESH,
            )
            for slot, (source, target) in enumerate(
                ((q_ref, rim_q), (k_ref, rim_k), (v_ref, rim_v))
            )
        ]

    @pl.when(has_after)
    def _():
        for copy in rim_copies():
            copy.start()

    @pl.when(jnp.logical_not(has_before))
    def _():
        rim_q[...] = jnp.zeros_like(rim_q)
        rim_k[...] = jnp.zeros_like(rim_k)
        rim_v[...] = jnp.zeros_like(rim_v)
        recv_s[...] = jnp.zeros_like(recv_s)

    row = lax.broadcasted_iota(jnp.int32, (HALF, HALF), 0)
    col = lax.broadcasted_iota(jnp.int32, (HALF, HALF), 1)
    for level in range(masks_s.shape[0]):
        wide = ((row >> (level + 1)) == (col >> (level + 1))) & (
            ((row >> level) & 1) == 1
        ) & (((col >> level) & 1) == 0)
        masks_s[level] = wide.astype(f32).astype(bf16)
    inclusive = row >= col
    strictly = row > col

    long_row = lax.broadcasted_iota(jnp.int32, (length, length), 0)
    long_col = lax.broadcasted_iota(jnp.int32, (length, length), 1)
    tril = (long_row >= long_col).astype(f32)
    eye = (long_row == long_col).astype(f32)
    highest = lax.Precision.HIGHEST
    decay_all = decay_ref[...]
    sums_row = dot_nt(decay_all, tril, highest)
    sums_col = dot_nt(tril, decay_all, highest)
    beta_col = dot_nt(eye, beta_ref[...], highest)
    for head in range(value_heads):
        ccol_s[head] = jnp.broadcast_to(sums_col[:, head : head + 1], (length, DK))
        bcol_s[head] = jnp.broadcast_to(beta_col[:, head : head + 1], (length, DK))
        crow_s[head] = jnp.broadcast_to(sums_row[head : head + 1, :], (8, length))

    @pl.when(has_before)
    def _():
        for copy in rim_copies():
            copy.wait_recv()

    def conv(ref, rim, taps_ref, columns, slot):
        conv_s[slot, 0:RIM, :] = rim[:, columns].astype(f32)
        conv_s[slot, RIM : RIM + length, :] = ref[:, columns].astype(f32)
        taps = taps_ref[:, columns].astype(f32)
        count = taps.shape[0]
        total = None
        for offset in range(count):
            first = RIM - count + 1 + offset
            term = taps[offset : offset + 1, :] * conv_s[slot, first : first + length, :]
            total = term if total is None else total + term
        return silu(total)

    def local(group, carry):
        columns = pl.ds(pl.multiple_of(group * DK, DK), DK)
        q = conv(q_ref, rim_q, cq_ref, columns, 0)
        k = conv(k_ref, rim_k, ck_ref, columns, 1)
        k = k * lax.rsqrt(jnp.sum(k * k, axis=-1, keepdims=True) + EPSILON)
        kb = k.astype(bf16)
        kk = dot_nt(kb, kb)
        qk = dot_nt(q.astype(bf16), kb)
        zero = jnp.zeros((HALF, HALF), f32)
        states = []
        systems = []
        for r in range(ratio):
            head = group * ratio + r
            v_columns = pl.ds(pl.multiple_of(head * DK, DK), DK)
            v = conv(v_ref, rim_v, cv_ref, v_columns, 2 + r)
            c = ccol_s[head]
            b = bcol_s[head]
            along = crow_s[head][0:1, :]
            d11 = jnp.exp(jnp.where(inclusive, c[:HALF] - along[:, :HALF], -1e30))
            d22 = jnp.exp(jnp.where(inclusive, c[HALF:] - along[:, HALF:], -1e30))
            d21 = jnp.exp(c[HALF:] - along[:, :HALF])
            l11 = jnp.where(strictly, b[:HALF] * d11 * kk[:HALF, :HALF], 0.0)
            l22 = jnp.where(strictly, b[HALF:] * d22 * kk[HALF:, HALF:], 0.0)
            l21 = b[HALF:] * d21 * kk[HALF:, :HALF]
            systems += [l11, l22]
            states.append((head, v, c, b, d11, d22, d21, l21))
        inverses = lower_inverses(systems, masks_s)
        for r in range(ratio):
            head, v, c, b, d11, d22, d21, l21 = states[r]
            x11, x22 = inverses[2 * r], inverses[2 * r + 1]
            x21 = -dot(x22, dot(l21, x11))
            inverse = jnp.concatenate(
                [jnp.concatenate([x11, zero], axis=1), jnp.concatenate([x21, x22], axis=1)], axis=0
            )
            e = jnp.exp(c)
            right = jnp.concatenate([b * v, b * e * k], axis=1)
            solved = dot(inverse, right).astype(bf16)
            attention = jnp.concatenate(
                [
                    jnp.concatenate([d11 * qk[:HALF, :HALF], zero], axis=1),
                    jnp.concatenate([d21 * qk[HALF:, :HALF], d22 * qk[HALF:, HALF:]], axis=1),
                ],
                axis=0,
            )
            seen = dot(attention, solved)
            local_s[head] = seen[:, :DK]
            couple_s[head] = (e * q - seen[:, DK:]).astype(bf16)
            last = c[length - 1 : length, :]
            moved = dot_tn(jnp.exp(last - c) * k, solved)
            inject_s[head] = moved[:, :DK]
            transit_s[head] = moved[:, DK:].astype(bf16)
            end_s[head] = jnp.broadcast_to(jnp.exp(last), (8, DK))
        return carry

    lax.fori_loop(0, key_heads, local, 0)

    def state_copy(head):
        return pltpu.make_async_remote_copy(
            src_ref=send_s.at[head],
            dst_ref=recv_s.at[head],
            send_sem=state_send.at[head],
            recv_sem=state_recv.at[head],
            device_id={"seq": after},
            device_id_type=MESH,
        )

    gain = gain_ref[...].astype(f32)

    def relay(head, carry):
        @pl.when(has_before)
        def _():
            state_copy(head).wait_recv()

        state = recv_s[head].astype(f32)
        held = state.astype(bf16)

        @pl.when(has_after)
        def _():
            following = (
                end_s[head][0:1, :] * state + inject_s[head] - dot(transit_s[head], held)
            )
            send_s[head] = following.astype(STATE)
            state_copy(head).start()

        core = local_s[head] + dot(couple_s[head], held)
        scale = lax.rsqrt(jnp.mean(core * core, axis=-1, keepdims=True) + EPSILON)
        columns = pl.ds(pl.multiple_of(head * DK, DK), DK)
        gate = g_ref[:, columns].astype(f32)
        hidden_s[:, columns] = (core * scale * gain * silu(gate)).astype(bf16)
        return carry

    lax.fori_loop(0, value_heads, relay, 0)
    w_copy.wait()

    chunks, _, rows, width = part_s.shape

    def part_copy(chunk, step):
        target = lax.rem(mine + step, head_count)
        return pltpu.make_async_remote_copy(
            src_ref=part_s.at[chunk, target],
            dst_ref=gather_s.at[chunk, step - 1],
            send_sem=part_send.at[chunk, step - 1],
            recv_sem=part_recv.at[chunk, step - 1],
            device_id={"head": target},
            device_id_type=MESH,
        )

    for chunk in range(chunks):
        product = jnp.dot(
            hidden_s[...],
            w_s[:, chunk * width : (chunk + 1) * width],
            preferred_element_type=f32,
        ).astype(bf16)
        for target in range(head_count):
            part_s[chunk, target] = product[target * rows : (target + 1) * rows]
        for step in range(1, head_count):
            part_copy(chunk, step).start()
    for chunk in range(chunks):
        total = part_s[chunk, mine].astype(f32)
        for step in range(1, head_count):
            part_copy(chunk, step).wait_recv()
            total = total + gather_s[chunk, step - 1].astype(f32)
        out_ref[:, chunk * width : (chunk + 1) * width] = total.astype(bf16)

    for chunk in range(chunks):
        for step in range(1, head_count):
            part_copy(chunk, step).wait_send()

    @pl.when(has_after)
    def _():
        for copy in rim_copies():
            copy.wait_send()
        for head in range(value_heads):
            state_copy(head).wait_send()


def shards(seq_count, head_count, *arrays):
    query_proj, key_proj, value_proj, gate_proj, strength, log_decay = arrays[:6]
    conv_query, conv_key, conv_value, norm_gain, out_weight = arrays[6:]
    length, key_cols = query_proj.shape
    value_cols = value_proj.shape[1]
    heads = value_cols // DK
    ratio = value_cols // key_cols
    width = out_weight.shape[1]
    rows = length // head_count
    chunks = width // CHUNK
    vmem = pl.BlockSpec(memory_space=pltpu.VMEM)
    others = head_count - 1
    return pl.pallas_call(
        functools.partial(kernel, seq_count, head_count),
        out_shape=jax.ShapeDtypeStruct((rows, width), bf16),
        in_specs=[vmem] * 10 + [pl.BlockSpec(memory_space=pl.ANY)],
        out_specs=vmem,
        scratch_shapes=[
            pltpu.VMEM((RIM, key_cols), bf16),
            pltpu.VMEM((RIM, key_cols), bf16),
            pltpu.VMEM((RIM, value_cols), bf16),
            pltpu.VMEM((2 + ratio, RIM + length, DK), f32),
            pltpu.VMEM((7, HALF, HALF), bf16),
            pltpu.VMEM((heads, length, DK), f32),
            pltpu.VMEM((heads, length, DK), f32),
            pltpu.VMEM((heads, 8, length), f32),
            pltpu.VMEM((heads, DK, DK), f32),
            pltpu.VMEM((heads, DK, DK), bf16),
            pltpu.VMEM((heads, 8, DK), f32),
            pltpu.VMEM((heads, length, DK), f32),
            pltpu.VMEM((heads, length, DK), bf16),
            pltpu.VMEM((heads, DK, DK), STATE),
            pltpu.VMEM((heads, DK, DK), STATE),
            pltpu.VMEM((length, value_cols), bf16),
            pltpu.VMEM((value_cols, width), bf16),
            pltpu.VMEM((chunks, head_count, rows, CHUNK), bf16),
            pltpu.VMEM((chunks, others, rows, CHUNK), bf16),
            pltpu.SemaphoreType.DMA,
            pltpu.SemaphoreType.DMA((3,)),
            pltpu.SemaphoreType.DMA((3,)),
            pltpu.SemaphoreType.DMA((heads,)),
            pltpu.SemaphoreType.DMA((heads,)),
            pltpu.SemaphoreType.DMA((chunks, others)),
            pltpu.SemaphoreType.DMA((chunks, others)),
        ],
        compiler_params=pltpu.CompilerParams(
            collective_id=0, has_side_effects=True, vmem_limit_bytes=48 * 1024 * 1024
        ),
    )(
        query_proj,
        key_proj,
        value_proj,
        gate_proj,
        strength,
        log_decay,
        conv_query,
        conv_key,
        conv_value,
        norm_gain.reshape(1, DK),
        out_weight,
    )


def solution(mesh):
    placed = (
        P("seq", "head"),
        P("seq", "head"),
        P("seq", "head"),
        P("seq", "head"),
        P("head", "seq"),
        P("head", "seq"),
        P(None, "head"),
        P(None, "head"),
        P(None, "head"),
        P(),
        P("head", None),
    )
    body = functools.partial(shards, mesh.shape["seq"], mesh.shape["head"])
    return jax.shard_map(
        body, mesh=mesh, in_specs=placed, out_specs=P(("seq", "head"), None), check_vma=False
    )
```

```python
import functools

import jax
import jax.numpy as jnp
from jax import lax
from jax.experimental import pallas as pl
from jax.experimental.pallas import tpu as pltpu
from jax.sharding import PartitionSpec as P

DK = 128
HALF = 128
RIM = 16
EPSILON = 1e-06
MESH = pl.DeviceIdType.MESH
f32 = jnp.float32
bf16 = jnp.bfloat16
CHUNK = 512
NOTE = 16


def dot(a, b):
    return jnp.dot(a.astype(bf16), b.astype(bf16), preferred_element_type=f32)


def dot_nt(a, b, precision=None):
    return lax.dot_general(
        a, b, (((1,), (1,)), ((), ())), precision=precision, preferred_element_type=f32
    )


def dot_tn(a, b):
    return lax.dot_general(
        a.astype(bf16), b.astype(bf16), (((0,), (0,)), ((), ())), preferred_element_type=f32
    )


def silu(x):
    return x / (1.0 + jnp.exp(-x))


def lower_inverses(systems, masks_ref):
    size = systems[0].shape[0]
    row = lax.broadcasted_iota(jnp.int32, (size, size), 0)
    col = lax.broadcasted_iota(jnp.int32, (size, size), 1)
    eye = (row == col).astype(f32)
    lows = [low.astype(bf16) for low in systems]
    inverses = [eye - (low * masks_ref[0]).astype(f32) for low in lows]
    for level in range(1, masks_ref.shape[0]):
        held = [inverse.astype(bf16) for inverse in inverses]
        inner = [dot(low * masks_ref[level], x) for low, x in zip(lows, held)]
        inverses = [old - dot(x, y) for old, x, y in zip(inverses, held, inner)]
    return inverses


def kernel(
    seq_count,
    head_count,
    q_hbm,
    k_hbm,
    v_hbm,
    g_hbm,
    beta_hbm,
    decay_hbm,
    cq_hbm,
    ck_hbm,
    cv_hbm,
    gain_hbm,
    w_hbm,
    out_ref,
    q_ref,
    k_ref,
    v_ref,
    g_ref,
    beta_ref,
    decay_ref,
    cq_ref,
    ck_ref,
    cv_ref,
    gain_ref,
    w_s,
    rim_q,
    rim_k,
    rim_v,
    conv_s,
    masks_s,
    ccol_s,
    bcol_s,
    crow_s,
    pair_s,
    inject_s,
    transit_s,
    end_s,
    local_s,
    couple_s,
    send_s,
    recv_s,
    hidden_s,
    part_s,
    near_s,
    sum_s,
    gather_s,
    load_sem,
    rim_send,
    rim_recv,
    pair_send,
    pair_recv,
    state_send,
    state_recv,
    near_send,
    near_recv,
    far_send,
    far_recv,
):
    me = lax.axis_index("seq")
    mine = lax.axis_index("head")
    length, key_cols = q_ref.shape
    key_heads = key_cols // DK
    value_heads = v_ref.shape[1] // DK
    ratio = value_heads // key_heads
    stages = seq_count // 2
    stage = lax.div(me, 2)
    parity = lax.rem(me, 2)
    columns_x = head_count // 2
    core = lax.rem(mine, 2)
    across = lax.div(mine, 2)
    has_before = me > 0
    has_after = me < seq_count - 1
    has_earlier = stage > 0
    has_later = stage < stages - 1
    after = lax.rem(me + 1, seq_count)
    before = lax.rem(me + seq_count - 1, seq_count)
    later = lax.rem(me + 2, seq_count)
    earlier = lax.rem(me + seq_count - 2, seq_count)
    partner = stage * 2 + 1 - parity
    twin = across * 2 + 1 - core

    def at_seq(index):
        return dict(device_id={"seq": index}, device_id_type=MESH)

    def at_head(index):
        return dict(device_id={"head": index}, device_id_type=MESH)

    loads = [
        pltpu.make_async_copy(source, target, load_sem.at[slot])
        for slot, (source, target) in enumerate(
            (
                (decay_hbm, decay_ref),
                (beta_hbm, beta_ref),
                (q_hbm, q_ref),
                (k_hbm, k_ref),
                (v_hbm, v_ref),
                (cq_hbm, cq_ref),
                (ck_hbm, ck_ref),
                (cv_hbm, cv_ref),
                (gain_hbm, gain_ref),
                (g_hbm, g_ref),
                (w_hbm, w_s),
            )
        )
    ]
    for load in loads:
        load.start()

    barrier = pltpu.get_barrier_semaphore()
    for there, index in (
        (has_before, before),
        (has_after, after),
        (has_earlier, earlier),
        (has_later, later),
    ):

        @pl.when(there)
        def _(index=index):
            pl.semaphore_signal(barrier, inc=1, **at_seq(index))

    pl.semaphore_signal(barrier, inc=1, **at_head(twin))
    for step in range(1, columns_x):
        other = lax.rem(across + step, columns_x) * 2 + core
        pl.semaphore_signal(barrier, inc=1, **at_head(other))
    greeted = columns_x
    for there in (has_before, has_after, has_earlier, has_later):
        greeted = greeted + there.astype(jnp.int32)
    pl.semaphore_wait(barrier, greeted)

    def rim_copies():
        return [
            pltpu.make_async_remote_copy(
                src_ref=source.at[pl.ds(length - RIM, RIM)],
                dst_ref=target,
                send_sem=rim_send.at[slot],
                recv_sem=rim_recv.at[slot],
                **at_seq(after),
            )
            for slot, (source, target) in enumerate(
                ((q_hbm, rim_q), (k_hbm, rim_k), (v_hbm, rim_v))
            )
        ]

    @pl.when(has_after)
    def _():
        for copy in rim_copies():
            copy.start()

    @pl.when(jnp.logical_not(has_before))
    def _():
        rim_q[...] = jnp.zeros_like(rim_q)
        rim_k[...] = jnp.zeros_like(rim_k)
        rim_v[...] = jnp.zeros_like(rim_v)

    @pl.when(jnp.logical_not(has_earlier))
    def _():
        recv_s[...] = jnp.zeros_like(recv_s)

    row = lax.broadcasted_iota(jnp.int32, (HALF, HALF), 0)
    col = lax.broadcasted_iota(jnp.int32, (HALF, HALF), 1)
    for level in range(masks_s.shape[0]):
        wide = ((row >> (level + 1)) == (col >> (level + 1))) & (
            ((row >> level) & 1) == 1
        ) & (((col >> level) & 1) == 0)
        masks_s[level] = wide.astype(f32).astype(bf16)

    loads[0].wait()
    loads[1].wait()
    long_row = lax.broadcasted_iota(jnp.int32, (length, length), 0)
    long_col = lax.broadcasted_iota(jnp.int32, (length, length), 1)
    tril = (long_row >= long_col).astype(f32)
    eye = (long_row == long_col).astype(f32)
    highest = lax.Precision.HIGHEST
    decay_all = decay_ref[...]
    sums_row = dot_nt(decay_all, tril, highest)
    sums_col = dot_nt(tril, decay_all, highest)
    beta_col = dot_nt(eye, beta_ref[...], highest)
    for head in range(value_heads):
        ccol_s[head] = jnp.broadcast_to(sums_col[:, head : head + 1], (length, DK))
        bcol_s[head] = jnp.broadcast_to(beta_col[:, head : head + 1], (length, DK))
        crow_s[head] = jnp.broadcast_to(sums_row[head : head + 1, :], (8, length))

    for load in loads[2:10]:
        load.wait()

    @pl.when(has_before)
    def _():
        for copy in rim_copies():
            copy.wait_recv()

    gain = gain_ref[...].astype(f32)

    def conv(ref, rim, taps_ref, columns, slot):
        conv_s[slot, 0:RIM, :] = rim[:, columns].astype(f32)
        conv_s[slot, RIM : RIM + length, :] = ref[:, columns].astype(f32)
        taps = taps_ref[:, columns].astype(f32)
        count = taps.shape[0]
        total = None
        for offset in range(count):
            first = RIM - count + 1 + offset
            term = taps[offset : offset + 1, :] * conv_s[slot, first : first + length, :]
            total = term if total is None else total + term
        return silu(total)

    def pair_copy(head):
        return pltpu.make_async_remote_copy(
            src_ref=pair_s.at[parity, head],
            dst_ref=pair_s.at[parity, head],
            send_sem=pair_send.at[head],
            recv_sem=pair_recv.at[head],
            **at_seq(partner),
        )

    def state_copy(head):
        return pltpu.make_async_remote_copy(
            src_ref=send_s.at[head],
            dst_ref=recv_s.at[head],
            send_sem=state_send.at[head],
            recv_sem=state_recv.at[head],
            **at_seq(later),
        )

    def local(group):
        inclusive = row >= col
        strictly = row > col
        columns = pl.ds(pl.multiple_of(group * DK, DK), DK)
        q = conv(q_ref, rim_q, cq_ref, columns, 0)
        k = conv(k_ref, rim_k, ck_ref, columns, 1)
        k = k * lax.rsqrt(jnp.sum(k * k, axis=-1, keepdims=True) + EPSILON)
        kb = k.astype(bf16)
        kk = dot_nt(kb, kb)
        qk = dot_nt(q.astype(bf16), kb)
        zero = jnp.zeros((HALF, HALF), f32)
        states = []
        systems = []
        for r in range(ratio):
            head = group * ratio + r
            v_columns = pl.ds(pl.multiple_of(head * DK, DK), DK)
            v = conv(v_ref, rim_v, cv_ref, v_columns, 2 + r)
            c = ccol_s[head]
            b = bcol_s[head]
            along = crow_s[head][0:1, :]
            d11 = jnp.exp(jnp.where(inclusive, c[:HALF] - along[:, :HALF], -1e30))
            d22 = jnp.exp(jnp.where(inclusive, c[HALF:] - along[:, HALF:], -1e30))
            d21 = jnp.exp(c[HALF:] - along[:, :HALF])
            l11 = jnp.where(strictly, b[:HALF] * d11 * kk[:HALF, :HALF], 0.0)
            l22 = jnp.where(strictly, b[HALF:] * d22 * kk[HALF:, HALF:], 0.0)
            l21 = b[HALF:] * d21 * kk[HALF:, :HALF]
            systems += [l11, l22]
            states.append((head, v, c, b, d11, d22, d21, l21))
        inverses = lower_inverses(systems, masks_s)
        for r in range(ratio):
            head, v, c, b, d11, d22, d21, l21 = states[r]
            x11, x22 = inverses[2 * r], inverses[2 * r + 1]
            x21 = -dot(x22, dot(l21, x11))
            inverse = jnp.concatenate(
                [jnp.concatenate([x11, zero], axis=1), jnp.concatenate([x21, x22], axis=1)], axis=0
            )
            e = jnp.exp(c)
            right = jnp.concatenate([b * v, b * e * k], axis=1)
            solved = dot(inverse, right).astype(bf16)
            last = c[length - 1 : length, :]
            moved = dot_tn(jnp.exp(last - c) * k, solved)
            pair_s[parity, head, 0:DK, :] = moved[:, DK:].astype(bf16)
            pair_s[parity, head, DK : 2 * DK, :] = moved[:, :DK].astype(bf16)
            end = jnp.broadcast_to(jnp.exp(last), (NOTE, DK))
            high = end.astype(bf16)
            rest = end - high.astype(f32)
            upper = lax.broadcasted_iota(jnp.int32, (NOTE, DK), 0) < NOTE // 2
            pair_s[parity, head, 2 * DK :, :] = jnp.where(upper, high.astype(f32), rest).astype(bf16)
            pair_copy(head).start()
            attention = jnp.concatenate(
                [
                    jnp.concatenate([d11 * qk[:HALF, :HALF], zero], axis=1),
                    jnp.concatenate([d21 * qk[HALF:, :HALF], d22 * qk[HALF:, HALF:]], axis=1),
                ],
                axis=0,
            )
            seen = dot(attention, solved)
            local_s[head] = seen[:, :DK]
            couple_s[head] = (e * q - seen[:, DK:]).astype(bf16)

    def unpacked(which, head):
        note = pair_s[which, head, 2 * DK :, :].astype(f32)
        end = note[0:1, :] + note[NOTE // 2 : NOTE // 2 + 1, :]
        return end, pair_s[which, head, 0:DK, :], pair_s[which, head, DK : 2 * DK, :]

    def compose(group):
        for r in range(ratio):
            pair_copy(group * ratio + r).wait_recv()
        for r in range(ratio):
            head = group * ratio + r
            end0, map0, inject0 = unpacked(0, head)
            end1, map1, inject1 = unpacked(1, head)
            both = dot(map1, jnp.concatenate([map0, inject0], axis=1))
            transit = end1 * map0.astype(f32) + end0 * map1.astype(f32) - both[:, :DK]
            transit_s[head] = transit.astype(bf16)
            inject_s[head] = end1 * inject0.astype(f32) + inject1.astype(f32) - both[:, DK:]
            end_s[head] = jnp.broadcast_to(end1 * end0, (8, DK))

    def relay(group):
        heads = [group * ratio + r for r in range(ratio)]

        @pl.when(has_earlier)
        def _():
            for head in heads:
                state_copy(head).wait_recv()

        @pl.when(has_later)
        def _():
            for head in heads:
                held = recv_s[head]
                following = (
                    end_s[head][0:1, :] * held.astype(f32)
                    + inject_s[head]
                    - dot(transit_s[head], held)
                )
                send_s[head] = following.astype(bf16)
                state_copy(head).start()

        odd = parity == 1
        for head in heads:
            held = recv_s[head]
            end0, map0, inject0 = unpacked(0, head)
            moved = end0 * held.astype(f32) + inject0.astype(f32) - dot(map0, held)
            state = jnp.where(odd, moved, held.astype(f32)).astype(bf16)
            core_out = local_s[head] + dot(couple_s[head], state)
            scale = lax.rsqrt(jnp.mean(core_out * core_out, axis=-1, keepdims=True) + EPSILON)
            columns = pl.ds(pl.multiple_of(head * DK, DK), DK)
            gate = g_ref[:, columns].astype(f32)
            hidden_s[:, columns] = (core_out * scale * gain * silu(gate)).astype(bf16)

    def slot(turn, carry):
        @pl.when(turn < key_heads)
        def _():
            local(turn)

        @pl.when((turn >= 1) & (turn <= key_heads))
        def _():
            compose(turn - 1)

        group = turn - 1 - stage

        @pl.when((group >= 0) & (group < key_heads))
        def _():
            relay(group)

        return carry

    lax.fori_loop(0, key_heads + stages, slot, 0)
    loads[10].wait()

    chunks, _, _, rows, width = part_s.shape

    def near_copy(chunk):
        return pltpu.make_async_remote_copy(
            src_ref=part_s.at[chunk, 1 - core],
            dst_ref=near_s.at[chunk],
            send_sem=near_send.at[chunk],
            recv_sem=near_recv.at[chunk],
            **at_head(twin),
        )

    def far_copy(chunk, step):
        target = lax.rem(across + step, columns_x)
        return pltpu.make_async_remote_copy(
            src_ref=sum_s.at[chunk, target],
            dst_ref=gather_s.at[chunk, step - 1],
            send_sem=far_send.at[chunk, step - 1],
            recv_sem=far_recv.at[chunk, step - 1],
            **at_head(target * 2 + core),
        )

    def project(chunk):
        product = jnp.dot(
            hidden_s[...],
            w_s[:, chunk * width : (chunk + 1) * width],
            preferred_element_type=f32,
        ).astype(bf16)
        for target in range(head_count):
            part_s[chunk, target % 2, target // 2] = product[target * rows : (target + 1) * rows]
        near_copy(chunk).start()

    def forward(chunk):
        near_copy(chunk).wait_recv()
        sum_s[chunk] = (part_s[chunk, core].astype(f32) + near_s[chunk].astype(f32)).astype(bf16)
        for step in range(1, columns_x):
            far_copy(chunk, step).start()

    lag = 2
    for turn in range(chunks + lag):
        if turn < chunks:
            project(turn)
        if turn >= lag:
            forward(turn - lag)
    for chunk in range(chunks):
        total = part_s[chunk, core, across].astype(f32) + near_s[chunk, across].astype(f32)
        for step in range(1, columns_x):
            far_copy(chunk, step).wait_recv()
            total = total + gather_s[chunk, step - 1].astype(f32)
        out_ref[:, chunk * width : (chunk + 1) * width] = total.astype(bf16)

    for chunk in range(chunks):
        near_copy(chunk).wait_send()
        for step in range(1, columns_x):
            far_copy(chunk, step).wait_send()
    for head in range(value_heads):
        pair_copy(head).wait_send()

    @pl.when(has_after)
    def _():
        for copy in rim_copies():
            copy.wait_send()

    @pl.when(has_later)
    def _():
        for head in range(value_heads):
            state_copy(head).wait_send()


def shards(seq_count, head_count, *arrays):
    query_proj, _, value_proj = arrays[:3]
    norm_gain, out_weight = arrays[9:]
    length, key_cols = query_proj.shape
    value_cols = value_proj.shape[1]
    heads = value_cols // DK
    ratio = value_cols // key_cols
    width = out_weight.shape[1]
    rows = length // head_count
    chunks = width // CHUNK
    operands = arrays[:9] + (norm_gain.reshape(1, DK), out_weight)
    columns_x = head_count // 2
    others = max(columns_x - 1, 1)
    semaphore = pltpu.SemaphoreType.DMA
    return pl.pallas_call(
        functools.partial(kernel, seq_count, head_count),
        out_shape=jax.ShapeDtypeStruct((rows, width), bf16),
        in_specs=[pl.BlockSpec(memory_space=pltpu.HBM)] * len(operands),
        out_specs=pl.BlockSpec(memory_space=pltpu.VMEM),
        scratch_shapes=[pltpu.VMEM(array.shape, array.dtype) for array in operands]
        + [
            pltpu.VMEM((RIM, key_cols), bf16),
            pltpu.VMEM((RIM, key_cols), bf16),
            pltpu.VMEM((RIM, value_cols), bf16),
            pltpu.VMEM((2 + ratio, RIM + length, DK), f32),
            pltpu.VMEM((7, HALF, HALF), bf16),
            pltpu.VMEM((heads, length, DK), f32),
            pltpu.VMEM((heads, length, DK), f32),
            pltpu.VMEM((heads, 8, length), f32),
            pltpu.VMEM((2, heads, 2 * DK + NOTE, DK), bf16),
            pltpu.VMEM((heads, DK, DK), f32),
            pltpu.VMEM((heads, DK, DK), bf16),
            pltpu.VMEM((heads, 8, DK), f32),
            pltpu.VMEM((heads, length, DK), f32),
            pltpu.VMEM((heads, length, DK), bf16),
            pltpu.VMEM((heads, DK, DK), bf16),
            pltpu.VMEM((heads, DK, DK), bf16),
            pltpu.VMEM((length, value_cols), bf16),
            pltpu.VMEM((chunks, 2, columns_x, rows, CHUNK), bf16),
            pltpu.VMEM((chunks, columns_x, rows, CHUNK), bf16),
            pltpu.VMEM((chunks, columns_x, rows, CHUNK), bf16),
            pltpu.VMEM((chunks, others, rows, CHUNK), bf16),
            semaphore((len(operands),)),
            semaphore((3,)),
            semaphore((3,)),
            semaphore((heads,)),
            semaphore((heads,)),
            semaphore((heads,)),
            semaphore((heads,)),
            semaphore((chunks,)),
            semaphore((chunks,)),
            semaphore((chunks, others)),
            semaphore((chunks, others)),
        ],
        compiler_params=pltpu.CompilerParams(
            collective_id=0, has_side_effects=True, vmem_limit_bytes=60 * 1024 * 1024
        ),
    )(*operands)


def solution(mesh):
    placed = (
        P("seq", "head"),
        P("seq", "head"),
        P("seq", "head"),
        P("seq", "head"),
        P("head", "seq"),
        P("head", "seq"),
        P(None, "head"),
        P(None, "head"),
        P(None, "head"),
        P(),
        P("head", None),
    )
    body = functools.partial(shards, mesh.shape["seq"], mesh.shape["head"])
    return jax.shard_map(
        body, mesh=mesh, in_specs=placed, out_specs=P(("seq", "head"), None), check_vma=False
    )
```

```python
import functools

import jax
import jax.numpy as jnp
from jax import lax
from jax.experimental import pallas as pl
from jax.experimental.pallas import tpu as pltpu
from jax.sharding import PartitionSpec as P

DK = 128
HALF = 128
RIM = 16
EPSILON = 1e-06
MESH = pl.DeviceIdType.MESH
f32 = jnp.float32
bf16 = jnp.bfloat16
CHUNK = 512
NOTE = 16


def dot(a, b):
    return jnp.dot(a.astype(bf16), b.astype(bf16), preferred_element_type=f32)


def dot_nt(a, b, precision=None):
    return lax.dot_general(
        a, b, (((1,), (1,)), ((), ())), precision=precision, preferred_element_type=f32
    )


def dot_tn(a, b):
    return lax.dot_general(
        a.astype(bf16), b.astype(bf16), (((0,), (0,)), ((), ())), preferred_element_type=f32
    )


def silu(x):
    return x / (1.0 + jnp.exp(-x))


def lower_inverses(systems, masks_ref):
    size = systems[0].shape[0]
    row = lax.broadcasted_iota(jnp.int32, (size, size), 0)
    col = lax.broadcasted_iota(jnp.int32, (size, size), 1)
    eye = (row == col).astype(f32)
    lows = [low.astype(bf16) for low in systems]
    inverses = [eye - (low * masks_ref[0]).astype(f32) for low in lows]
    for level in range(1, masks_ref.shape[0]):
        held = [inverse.astype(bf16) for inverse in inverses]
        inner = [dot(low * masks_ref[level], x) for low, x in zip(lows, held)]
        inverses = [old - dot(x, y) for old, x, y in zip(inverses, held, inner)]
    return inverses


def kernel(
    seq_count,
    head_count,
    q_hbm,
    k_hbm,
    v_hbm,
    g_hbm,
    beta_hbm,
    decay_hbm,
    cq_hbm,
    ck_hbm,
    cv_hbm,
    gain_hbm,
    w_hbm,
    out_ref,
    q_ref,
    k_ref,
    v_ref,
    g_ref,
    beta_ref,
    decay_ref,
    cq_ref,
    ck_ref,
    cv_ref,
    gain_ref,
    w_s,
    rim_q,
    rim_k,
    rim_v,
    conv_s,
    masks_s,
    ccol_s,
    bcol_s,
    crow_s,
    pair_s,
    inject_s,
    transit_s,
    end_s,
    local_s,
    couple_s,
    attention_s,
    solved_s,
    send_s,
    recv_s,
    hidden_s,
    part_s,
    near_s,
    sum_s,
    gather_s,
    load_sem,
    rim_send,
    rim_recv,
    pair_send,
    pair_recv,
    state_send,
    state_recv,
    near_send,
    near_recv,
    far_send,
    far_recv,
):
    me = lax.axis_index("seq")
    mine = lax.axis_index("head")
    length, key_cols = q_ref.shape
    key_heads = key_cols // DK
    value_heads = v_ref.shape[1] // DK
    ratio = value_heads // key_heads
    stages = seq_count // 2
    stage = lax.div(me, 2)
    parity = lax.rem(me, 2)
    columns_x = head_count // 2
    core = lax.rem(mine, 2)
    across = lax.div(mine, 2)
    has_before = me > 0
    has_after = me < seq_count - 1
    has_earlier = stage > 0
    has_later = stage < stages - 1
    after = lax.rem(me + 1, seq_count)
    before = lax.rem(me + seq_count - 1, seq_count)
    later = lax.rem(me + 2, seq_count)
    earlier = lax.rem(me + seq_count - 2, seq_count)
    partner = stage * 2 + 1 - parity
    twin = across * 2 + 1 - core

    def at_seq(index):
        return dict(device_id={"seq": index}, device_id_type=MESH)

    def at_head(index):
        return dict(device_id={"head": index}, device_id_type=MESH)

    loads = [
        pltpu.make_async_copy(source, target, load_sem.at[slot])
        for slot, (source, target) in enumerate(
            (
                (decay_hbm, decay_ref),
                (beta_hbm, beta_ref),
                (q_hbm, q_ref),
                (k_hbm, k_ref),
                (v_hbm, v_ref),
                (cq_hbm, cq_ref),
                (ck_hbm, ck_ref),
                (cv_hbm, cv_ref),
                (gain_hbm, gain_ref),
                (g_hbm, g_ref),
                (w_hbm, w_s),
            )
        )
    ]
    for load in loads:
        load.start()

    barrier = pltpu.get_barrier_semaphore()
    for there, index in (
        (has_before, before),
        (has_after, after),
        (has_earlier, earlier),
        (has_later, later),
    ):

        @pl.when(there)
        def _(index=index):
            pl.semaphore_signal(barrier, inc=1, **at_seq(index))

    pl.semaphore_signal(barrier, inc=1, **at_head(twin))
    for step in range(1, columns_x):
        other = lax.rem(across + step, columns_x) * 2 + core
        pl.semaphore_signal(barrier, inc=1, **at_head(other))
    greeted = columns_x
    for there in (has_before, has_after, has_earlier, has_later):
        greeted = greeted + there.astype(jnp.int32)
    row = lax.broadcasted_iota(jnp.int32, (HALF, HALF), 0)
    col = lax.broadcasted_iota(jnp.int32, (HALF, HALF), 1)
    for level in range(masks_s.shape[0]):
        wide = ((row >> (level + 1)) == (col >> (level + 1))) & (
            ((row >> level) & 1) == 1
        ) & (((col >> level) & 1) == 0)
        masks_s[level] = wide.astype(f32).astype(bf16)

    pl.semaphore_wait(barrier, greeted)

    def rim_copies():
        return [
            pltpu.make_async_remote_copy(
                src_ref=source.at[pl.ds(length - RIM, RIM)],
                dst_ref=target,
                send_sem=rim_send.at[slot],
                recv_sem=rim_recv.at[slot],
                **at_seq(after),
            )
            for slot, (source, target) in enumerate(
                ((q_hbm, rim_q), (k_hbm, rim_k), (v_hbm, rim_v))
            )
        ]

    @pl.when(has_after)
    def _():
        for copy in rim_copies():
            copy.start()

    @pl.when(jnp.logical_not(has_before))
    def _():
        rim_q[...] = jnp.zeros_like(rim_q)
        rim_k[...] = jnp.zeros_like(rim_k)
        rim_v[...] = jnp.zeros_like(rim_v)

    @pl.when(jnp.logical_not(has_earlier))
    def _():
        recv_s[...] = jnp.zeros_like(recv_s)

    loads[0].wait()
    loads[1].wait()
    long_row = lax.broadcasted_iota(jnp.int32, (length, length), 0)
    long_col = lax.broadcasted_iota(jnp.int32, (length, length), 1)
    tril = (long_row >= long_col).astype(f32)
    eye = (long_row == long_col).astype(f32)
    highest = lax.Precision.HIGHEST
    decay_all = decay_ref[...]
    sums_row = dot_nt(decay_all, tril, highest)
    sums_col = dot_nt(tril, decay_all, highest)
    beta_col = dot_nt(eye, beta_ref[...], highest)
    for head in range(value_heads):
        ccol_s[head] = jnp.broadcast_to(sums_col[:, head : head + 1], (length, DK))
        bcol_s[head] = jnp.broadcast_to(beta_col[:, head : head + 1], (length, DK))
        crow_s[head] = jnp.broadcast_to(sums_row[head : head + 1, :], (8, length))

    for load in loads[2:10]:
        load.wait()

    @pl.when(has_before)
    def _():
        for copy in rim_copies():
            copy.wait_recv()

    gain = gain_ref[...].astype(f32)

    def conv(ref, rim, taps_ref, columns, slot):
        conv_s[slot, 0:RIM, :] = rim[:, columns].astype(f32)
        conv_s[slot, RIM : RIM + length, :] = ref[:, columns].astype(f32)
        taps = taps_ref[:, columns].astype(f32)
        count = taps.shape[0]
        total = None
        for offset in range(count):
            first = RIM - count + 1 + offset
            term = taps[offset : offset + 1, :] * conv_s[slot, first : first + length, :]
            total = term if total is None else total + term
        return silu(total)

    def pair_copy(head):
        return pltpu.make_async_remote_copy(
            src_ref=pair_s.at[parity, head],
            dst_ref=pair_s.at[parity, head],
            send_sem=pair_send.at[head],
            recv_sem=pair_recv.at[head],
            **at_seq(partner),
        )

    def state_copy(head):
        return pltpu.make_async_remote_copy(
            src_ref=send_s.at[head],
            dst_ref=recv_s.at[head],
            send_sem=state_send.at[head],
            recv_sem=state_recv.at[head],
            **at_seq(later),
        )

    def local(group):
        inclusive = row >= col
        strictly = row > col
        columns = pl.ds(pl.multiple_of(group * DK, DK), DK)
        q = conv(q_ref, rim_q, cq_ref, columns, 0)
        k = conv(k_ref, rim_k, ck_ref, columns, 1)
        k = k * lax.rsqrt(jnp.sum(k * k, axis=-1, keepdims=True) + EPSILON)
        kb = k.astype(bf16)
        kk = dot_nt(kb, kb)
        qk = dot_nt(q.astype(bf16), kb)
        zero = jnp.zeros((HALF, HALF), f32)
        states = []
        systems = []
        for r in range(ratio):
            head = group * ratio + r
            v_columns = pl.ds(pl.multiple_of(head * DK, DK), DK)
            v = conv(v_ref, rim_v, cv_ref, v_columns, 2 + r)
            c = ccol_s[head]
            b = bcol_s[head]
            along = crow_s[head][0:1, :]
            d11 = jnp.exp(jnp.where(inclusive, c[:HALF] - along[:, :HALF], -1e30))
            d22 = jnp.exp(jnp.where(inclusive, c[HALF:] - along[:, HALF:], -1e30))
            d21 = jnp.exp(c[HALF:] - along[:, :HALF])
            l11 = jnp.where(strictly, b[:HALF] * d11 * kk[:HALF, :HALF], 0.0)
            l22 = jnp.where(strictly, b[HALF:] * d22 * kk[HALF:, HALF:], 0.0)
            l21 = b[HALF:] * d21 * kk[HALF:, :HALF]
            systems += [l11, l22]
            states.append((head, v, c, b, d11, d22, d21, l21))
        inverses = lower_inverses(systems, masks_s)
        for r in range(ratio):
            head, v, c, b, d11, d22, d21, l21 = states[r]
            x11, x22 = inverses[2 * r], inverses[2 * r + 1]
            x21 = -dot(x22, dot(l21, x11))
            inverse = jnp.concatenate(
                [jnp.concatenate([x11, zero], axis=1), jnp.concatenate([x21, x22], axis=1)], axis=0
            )
            e = jnp.exp(c)
            right = jnp.concatenate([b * v, b * e * k], axis=1)
            solved = dot(inverse, right).astype(bf16)
            last = c[length - 1 : length, :]
            moved = dot_tn(jnp.exp(last - c) * k, solved)
            pair_s[parity, head, 0:DK, :] = moved[:, DK:].astype(bf16)
            pair_s[parity, head, DK : 2 * DK, :] = moved[:, :DK].astype(bf16)
            end = jnp.broadcast_to(jnp.exp(last), (NOTE, DK))
            high = end.astype(bf16)
            rest = end - high.astype(f32)
            upper = lax.broadcasted_iota(jnp.int32, (NOTE, DK), 0) < NOTE // 2
            pair_s[parity, head, 2 * DK :, :] = jnp.where(upper, high.astype(f32), rest).astype(bf16)
            pair_copy(head).start()
            attention_s[head] = jnp.concatenate(
                [
                    jnp.concatenate([d11 * qk[:HALF, :HALF], zero], axis=1),
                    jnp.concatenate([d21 * qk[HALF:, :HALF], d22 * qk[HALF:, HALF:]], axis=1),
                ],
                axis=0,
            ).astype(bf16)
            solved_s[head] = solved
            couple_s[head] = (e * q).astype(f32)

    def attend(group):
        for r in range(ratio):
            head = group * ratio + r
            seen = dot(attention_s[head], solved_s[head])
            local_s[head] = seen[:, :DK]
            couple_s[head] = couple_s[head] - seen[:, DK:]

    def unpacked(which, head):
        note = pair_s[which, head, 2 * DK :, :].astype(f32)
        end = note[0:1, :] + note[NOTE // 2 : NOTE // 2 + 1, :]
        return end, pair_s[which, head, 0:DK, :], pair_s[which, head, DK : 2 * DK, :]

    def compose(group):
        for r in range(ratio):
            head = group * ratio + r
            pair_copy(head).wait_recv()
            end0, map0, inject0 = unpacked(0, head)
            end1, map1, inject1 = unpacked(1, head)
            both = dot(map1, jnp.concatenate([map0, inject0], axis=1))
            transit = end1 * map0.astype(f32) + end0 * map1.astype(f32) - both[:, :DK]
            transit_s[head] = transit.astype(bf16)
            inject_s[head] = end1 * inject0.astype(f32) + inject1.astype(f32) - both[:, DK:]
            end_s[head] = jnp.broadcast_to(end1 * end0, (8, DK))

            @pl.when(has_later & jnp.logical_not(has_earlier))
            def _(head=head):
                send_s[head] = inject_s[head].astype(bf16)
                state_copy(head).start()

    def relay(group, waits):
        heads = [group * ratio + r for r in range(ratio)]

        for head in heads:
            if waits:
                state_copy(head).wait_recv()

            if waits:

                @pl.when(has_later)
                def _(head=head):
                    held = recv_s[head]
                    following = (
                        end_s[head][0:1, :] * held.astype(f32)
                        + inject_s[head]
                        - dot(transit_s[head], held)
                    )
                    send_s[head] = following.astype(bf16)
                    state_copy(head).start()

        odd = parity == 1
        for head in heads:
            held = recv_s[head]
            end0, map0, inject0 = unpacked(0, head)
            moved = end0 * held.astype(f32) + inject0.astype(f32) - dot(map0, held)
            state = jnp.where(odd, moved, held.astype(f32)).astype(bf16)
            core_out = local_s[head] + dot(couple_s[head], state)
            scale = lax.rsqrt(jnp.mean(core_out * core_out, axis=-1, keepdims=True) + EPSILON)
            columns = pl.ds(pl.multiple_of(head * DK, DK), DK)
            gate = g_ref[:, columns].astype(f32)
            hidden_s[:, columns] = (core_out * scale * gain * silu(gate)).astype(bf16)

    def slot(turn, carry):
        @pl.when(turn < key_heads)
        def _():
            local(turn)

        composing = (turn >= 1) & (turn <= key_heads)
        group = turn - 1 - stage
        relaying = (group >= 0) & (group < key_heads)

        @pl.when(composing)
        def _():
            attend(turn - 1)

        @pl.when(relaying & has_earlier)
        def _():
            relay(group, True)

        @pl.when(composing)
        def _():
            compose(turn - 1)

        @pl.when(relaying & jnp.logical_not(has_earlier))
        def _():
            relay(group, False)

        return carry

    lax.fori_loop(0, key_heads + stages, slot, 0)
    loads[10].wait()

    chunks, _, _, rows, width = part_s.shape

    def near_copy(chunk):
        return pltpu.make_async_remote_copy(
            src_ref=part_s.at[chunk, 1 - core],
            dst_ref=near_s.at[chunk],
            send_sem=near_send.at[chunk],
            recv_sem=near_recv.at[chunk],
            **at_head(twin),
        )

    def far_copy(chunk, step):
        target = lax.rem(across + step, columns_x)
        return pltpu.make_async_remote_copy(
            src_ref=sum_s.at[chunk, target],
            dst_ref=gather_s.at[chunk, step - 1],
            send_sem=far_send.at[chunk, step - 1],
            recv_sem=far_recv.at[chunk, step - 1],
            **at_head(target * 2 + core),
        )

    def project(chunk):
        product = jnp.dot(
            hidden_s[...],
            w_s[:, chunk * width : (chunk + 1) * width],
            preferred_element_type=f32,
        ).astype(bf16)
        for target in range(head_count):
            part_s[chunk, target % 2, target // 2] = product[target * rows : (target + 1) * rows]
        near_copy(chunk).start()

    def forward(chunk):
        near_copy(chunk).wait_recv()
        sum_s[chunk] = (part_s[chunk, core].astype(f32) + near_s[chunk].astype(f32)).astype(bf16)
        for step in range(1, columns_x):
            far_copy(chunk, step).start()

    lag = 2
    for turn in range(chunks + lag):
        if turn < chunks:
            project(turn)
        if turn >= lag:
            forward(turn - lag)
    for chunk in range(chunks):
        total = part_s[chunk, core, across].astype(f32) + near_s[chunk, across].astype(f32)
        for step in range(1, columns_x):
            far_copy(chunk, step).wait_recv()
            total = total + gather_s[chunk, step - 1].astype(f32)
        out_ref[:, chunk * width : (chunk + 1) * width] = total.astype(bf16)

    for chunk in range(chunks):
        near_copy(chunk).wait_send()
        for step in range(1, columns_x):
            far_copy(chunk, step).wait_send()
    for head in range(value_heads):
        pair_copy(head).wait_send()

    @pl.when(has_after)
    def _():
        for copy in rim_copies():
            copy.wait_send()

    @pl.when(has_later)
    def _():
        for head in range(value_heads):
            state_copy(head).wait_send()


def shards(seq_count, head_count, *arrays):
    query_proj, _, value_proj = arrays[:3]
    norm_gain, out_weight = arrays[9:]
    length, key_cols = query_proj.shape
    value_cols = value_proj.shape[1]
    heads = value_cols // DK
    ratio = value_cols // key_cols
    width = out_weight.shape[1]
    rows = length // head_count
    chunks = width // CHUNK
    operands = arrays[:9] + (norm_gain.reshape(1, DK), out_weight)
    columns_x = head_count // 2
    others = max(columns_x - 1, 1)
    semaphore = pltpu.SemaphoreType.DMA
    return pl.pallas_call(
        functools.partial(kernel, seq_count, head_count),
        out_shape=jax.ShapeDtypeStruct((rows, width), bf16),
        in_specs=[pl.BlockSpec(memory_space=pltpu.HBM)] * len(operands),
        out_specs=pl.BlockSpec(memory_space=pltpu.VMEM),
        scratch_shapes=[pltpu.VMEM(array.shape, array.dtype) for array in operands]
        + [
            pltpu.VMEM((RIM, key_cols), bf16),
            pltpu.VMEM((RIM, key_cols), bf16),
            pltpu.VMEM((RIM, value_cols), bf16),
            pltpu.VMEM((2 + ratio, RIM + length, DK), f32),
            pltpu.VMEM((7, HALF, HALF), bf16),
            pltpu.VMEM((heads, length, DK), f32),
            pltpu.VMEM((heads, length, DK), f32),
            pltpu.VMEM((heads, 8, length), f32),
            pltpu.VMEM((2, heads, 2 * DK + NOTE, DK), bf16),
            pltpu.VMEM((heads, DK, DK), f32),
            pltpu.VMEM((heads, DK, DK), bf16),
            pltpu.VMEM((heads, 8, DK), f32),
            pltpu.VMEM((heads, length, DK), f32),
            pltpu.VMEM((heads, length, DK), f32),
            pltpu.VMEM((heads, length, length), bf16),
            pltpu.VMEM((heads, length, 2 * DK), bf16),
            pltpu.VMEM((heads, DK, DK), bf16),
            pltpu.VMEM((heads, DK, DK), bf16),
            pltpu.VMEM((length, value_cols), bf16),
            pltpu.VMEM((chunks, 2, columns_x, rows, CHUNK), bf16),
            pltpu.VMEM((chunks, columns_x, rows, CHUNK), bf16),
            pltpu.VMEM((chunks, columns_x, rows, CHUNK), bf16),
            pltpu.VMEM((chunks, others, rows, CHUNK), bf16),
            semaphore((len(operands),)),
            semaphore((3,)),
            semaphore((3,)),
            semaphore((heads,)),
            semaphore((heads,)),
            semaphore((heads,)),
            semaphore((heads,)),
            semaphore((chunks,)),
            semaphore((chunks,)),
            semaphore((chunks, others)),
            semaphore((chunks, others)),
        ],
        compiler_params=pltpu.CompilerParams(
            collective_id=0, has_side_effects=True, vmem_limit_bytes=60 * 1024 * 1024
        ),
    )(*operands)


def solution(mesh):
    placed = (
        P("seq", "head"),
        P("seq", "head"),
        P("seq", "head"),
        P("seq", "head"),
        P("head", "seq"),
        P("head", "seq"),
        P(None, "head"),
        P(None, "head"),
        P(None, "head"),
        P(),
        P("head", None),
    )
    body = functools.partial(shards, mesh.shape["seq"], mesh.shape["head"])
    return jax.shard_map(
        body, mesh=mesh, in_specs=placed, out_specs=P(("seq", "head"), None), check_vma=False
    )
```

```python
import functools

import jax
import jax.numpy as jnp
from jax import lax
from jax.experimental import pallas as pl
from jax.experimental.pallas import tpu as pltpu
from jax.sharding import PartitionSpec as P

DK = 128
HALF = 128
RIM = 16
EPSILON = 1e-06
MESH = pl.DeviceIdType.MESH
f32 = jnp.float32
bf16 = jnp.bfloat16
CHUNK = 256
NOTE = 16


def dot(a, b):
    return jnp.dot(a.astype(bf16), b.astype(bf16), preferred_element_type=f32)


def dot_nt(a, b, precision=None):
    return lax.dot_general(
        a, b, (((1,), (1,)), ((), ())), precision=precision, preferred_element_type=f32
    )


def dot_tn(a, b):
    return lax.dot_general(
        a.astype(bf16), b.astype(bf16), (((0,), (0,)), ((), ())), preferred_element_type=f32
    )


def silu(x):
    return x / (1.0 + jnp.exp(-x))


def lower_inverses(systems, masks_ref):
    size = systems[0].shape[0]
    row = lax.broadcasted_iota(jnp.int32, (size, size), 0)
    col = lax.broadcasted_iota(jnp.int32, (size, size), 1)
    eye = (row == col).astype(f32)
    lows = [low.astype(bf16) for low in systems]
    inverses = [eye - (low * masks_ref[0]).astype(f32) for low in lows]
    for level in range(1, masks_ref.shape[0]):
        held = [inverse.astype(bf16) for inverse in inverses]
        inner = [dot(low * masks_ref[level], x) for low, x in zip(lows, held)]
        inverses = [old - dot(x, y) for old, x, y in zip(inverses, held, inner)]
    return inverses


def kernel(
    seq_count,
    head_count,
    q_hbm,
    k_hbm,
    v_hbm,
    g_hbm,
    beta_hbm,
    decay_hbm,
    cq_hbm,
    ck_hbm,
    cv_hbm,
    gain_hbm,
    w_hbm,
    out_ref,
    q_ref,
    k_ref,
    v_ref,
    g_ref,
    beta_ref,
    decay_ref,
    cq_ref,
    ck_ref,
    cv_ref,
    gain_ref,
    w_s,
    rim_q,
    rim_k,
    rim_v,
    conv_s,
    masks_s,
    ccol_s,
    bcol_s,
    crow_s,
    pair_s,
    inject_s,
    transit_s,
    end_s,
    local_s,
    couple_s,
    attention_s,
    solved_s,
    send_s,
    recv_s,
    hidden_s,
    part_s,
    near_s,
    sum_s,
    gather_s,
    load_sem,
    rim_send,
    rim_recv,
    pair_send,
    pair_recv,
    state_send,
    state_recv,
    near_send,
    near_recv,
    far_send,
    far_recv,
):
    me = lax.axis_index("seq")
    mine = lax.axis_index("head")
    length, key_cols = q_ref.shape
    key_heads = key_cols // DK
    value_heads = v_ref.shape[1] // DK
    ratio = value_heads // key_heads
    stages = seq_count // 2
    stage = lax.div(me, 2)
    parity = lax.rem(me, 2)
    columns_x = head_count // 2
    core = lax.rem(mine, 2)
    across = lax.div(mine, 2)
    has_before = me > 0
    has_after = me < seq_count - 1
    has_earlier = stage > 0
    has_later = stage < stages - 1
    after = lax.rem(me + 1, seq_count)
    before = lax.rem(me + seq_count - 1, seq_count)
    later = lax.rem(me + 2, seq_count)
    earlier = lax.rem(me + seq_count - 2, seq_count)
    partner = stage * 2 + 1 - parity
    twin = across * 2 + 1 - core

    def at_seq(index):
        return dict(device_id={"seq": index}, device_id_type=MESH)

    def at_head(index):
        return dict(device_id={"head": index}, device_id_type=MESH)

    loads = [
        pltpu.make_async_copy(source, target, load_sem.at[slot])
        for slot, (source, target) in enumerate(
            (
                (decay_hbm, decay_ref),
                (beta_hbm, beta_ref),
                (q_hbm, q_ref),
                (k_hbm, k_ref),
                (v_hbm, v_ref),
                (cq_hbm, cq_ref),
                (ck_hbm, ck_ref),
                (cv_hbm, cv_ref),
                (gain_hbm, gain_ref),
                (g_hbm, g_ref),
                (w_hbm, w_s),
            )
        )
    ]
    for load in loads:
        load.start()

    barrier = pltpu.get_barrier_semaphore()
    for there, index in (
        (has_before, before),
        (has_after, after),
        (has_earlier, earlier),
        (has_later, later),
    ):

        @pl.when(there)
        def _(index=index):
            pl.semaphore_signal(barrier, inc=1, **at_seq(index))

    pl.semaphore_signal(barrier, inc=1, **at_head(twin))
    for step in range(1, columns_x):
        other = lax.rem(across + step, columns_x) * 2 + core
        pl.semaphore_signal(barrier, inc=1, **at_head(other))
    greeted = columns_x
    for there in (has_before, has_after, has_earlier, has_later):
        greeted = greeted + there.astype(jnp.int32)
    row = lax.broadcasted_iota(jnp.int32, (HALF, HALF), 0)
    col = lax.broadcasted_iota(jnp.int32, (HALF, HALF), 1)
    for level in range(masks_s.shape[0]):
        wide = ((row >> (level + 1)) == (col >> (level + 1))) & (
            ((row >> level) & 1) == 1
        ) & (((col >> level) & 1) == 0)
        masks_s[level] = wide.astype(f32).astype(bf16)

    pl.semaphore_wait(barrier, greeted)

    def rim_copies():
        return [
            pltpu.make_async_remote_copy(
                src_ref=source.at[pl.ds(length - RIM, RIM)],
                dst_ref=target,
                send_sem=rim_send.at[slot],
                recv_sem=rim_recv.at[slot],
                **at_seq(after),
            )
            for slot, (source, target) in enumerate(
                ((q_hbm, rim_q), (k_hbm, rim_k), (v_hbm, rim_v))
            )
        ]

    @pl.when(has_after)
    def _():
        for copy in rim_copies():
            copy.start()

    @pl.when(jnp.logical_not(has_before))
    def _():
        rim_q[...] = jnp.zeros_like(rim_q)
        rim_k[...] = jnp.zeros_like(rim_k)
        rim_v[...] = jnp.zeros_like(rim_v)

    @pl.when(jnp.logical_not(has_earlier))
    def _():
        recv_s[...] = jnp.zeros_like(recv_s)

    loads[0].wait()
    loads[1].wait()
    long_row = lax.broadcasted_iota(jnp.int32, (length, length), 0)
    long_col = lax.broadcasted_iota(jnp.int32, (length, length), 1)
    tril = (long_row >= long_col).astype(f32)
    eye = (long_row == long_col).astype(f32)
    highest = lax.Precision.HIGHEST
    decay_all = decay_ref[...]
    sums_row = dot_nt(decay_all, tril, highest)
    sums_col = dot_nt(tril, decay_all, highest)
    beta_col = dot_nt(eye, beta_ref[...], highest)
    for head in range(value_heads):
        ccol_s[head] = jnp.broadcast_to(sums_col[:, head : head + 1], (length, DK))
        bcol_s[head] = jnp.broadcast_to(beta_col[:, head : head + 1], (length, DK))
        crow_s[head] = jnp.broadcast_to(sums_row[head : head + 1, :], (8, length))

    for load in loads[2:10]:
        load.wait()

    @pl.when(has_before)
    def _():
        for copy in rim_copies():
            copy.wait_recv()

    gain = gain_ref[...].astype(f32)

    def conv(ref, rim, taps_ref, columns, slot):
        conv_s[slot, 0:RIM, :] = rim[:, columns].astype(f32)
        conv_s[slot, RIM : RIM + length, :] = ref[:, columns].astype(f32)
        taps = taps_ref[:, columns].astype(f32)
        count = taps.shape[0]
        total = None
        for offset in range(count):
            first = RIM - count + 1 + offset
            term = taps[offset : offset + 1, :] * conv_s[slot, first : first + length, :]
            total = term if total is None else total + term
        return silu(total)

    def pair_copy(head):
        return pltpu.make_async_remote_copy(
            src_ref=pair_s.at[parity, head],
            dst_ref=pair_s.at[parity, head],
            send_sem=pair_send.at[head],
            recv_sem=pair_recv.at[head],
            **at_seq(partner),
        )

    def state_copy(head):
        return pltpu.make_async_remote_copy(
            src_ref=send_s.at[head],
            dst_ref=recv_s.at[head],
            send_sem=state_send.at[head],
            recv_sem=state_recv.at[head],
            **at_seq(later),
        )

    def local(group):
        inclusive = row >= col
        strictly = row > col
        columns = pl.ds(pl.multiple_of(group * DK, DK), DK)
        q = conv(q_ref, rim_q, cq_ref, columns, 0)
        k = conv(k_ref, rim_k, ck_ref, columns, 1)
        k = k * lax.rsqrt(jnp.sum(k * k, axis=-1, keepdims=True) + EPSILON)
        kb = k.astype(bf16)
        kk = dot_nt(kb, kb)
        qk = dot_nt(q.astype(bf16), kb)
        zero = jnp.zeros((HALF, HALF), f32)
        states = []
        systems = []
        for r in range(ratio):
            head = group * ratio + r
            v_columns = pl.ds(pl.multiple_of(head * DK, DK), DK)
            v = conv(v_ref, rim_v, cv_ref, v_columns, 2 + r)
            c = ccol_s[head]
            b = bcol_s[head]
            along = crow_s[head][0:1, :]
            d11 = jnp.exp(jnp.where(inclusive, c[:HALF] - along[:, :HALF], -1e30))
            d22 = jnp.exp(jnp.where(inclusive, c[HALF:] - along[:, HALF:], -1e30))
            d21 = jnp.exp(c[HALF:] - along[:, :HALF])
            l11 = jnp.where(strictly, b[:HALF] * d11 * kk[:HALF, :HALF], 0.0)
            l22 = jnp.where(strictly, b[HALF:] * d22 * kk[HALF:, HALF:], 0.0)
            l21 = b[HALF:] * d21 * kk[HALF:, :HALF]
            systems += [l11, l22]
            states.append((head, v, c, b, d11, d22, d21, l21))
        inverses = lower_inverses(systems, masks_s)
        for r in range(ratio):
            head, v, c, b, d11, d22, d21, l21 = states[r]
            x11, x22 = inverses[2 * r], inverses[2 * r + 1]
            x21 = -dot(x22, dot(l21, x11))
            inverse = jnp.concatenate(
                [jnp.concatenate([x11, zero], axis=1), jnp.concatenate([x21, x22], axis=1)], axis=0
            )
            e = jnp.exp(c)
            right = jnp.concatenate([b * v, b * e * k], axis=1)
            solved = dot(inverse, right).astype(bf16)
            last = c[length - 1 : length, :]
            moved = dot_tn(jnp.exp(last - c) * k, solved)
            pair_s[parity, head, 0:DK, :] = moved[:, DK:].astype(bf16)
            pair_s[parity, head, DK : 2 * DK, :] = moved[:, :DK].astype(bf16)
            end = jnp.broadcast_to(jnp.exp(last), (NOTE, DK))
            high = end.astype(bf16)
            rest = end - high.astype(f32)
            upper = lax.broadcasted_iota(jnp.int32, (NOTE, DK), 0) < NOTE // 2
            pair_s[parity, head, 2 * DK :, :] = jnp.where(upper, high.astype(f32), rest).astype(bf16)
            pair_copy(head).start()
            attention_s[head] = jnp.concatenate(
                [
                    jnp.concatenate([d11 * qk[:HALF, :HALF], zero], axis=1),
                    jnp.concatenate([d21 * qk[HALF:, :HALF], d22 * qk[HALF:, HALF:]], axis=1),
                ],
                axis=0,
            ).astype(bf16)
            solved_s[head] = solved
            couple_s[head] = (e * q).astype(f32)

    def attend(group):
        for r in range(ratio):
            head = group * ratio + r
            seen = dot(attention_s[head], solved_s[head])
            local_s[head] = seen[:, :DK]
            couple_s[head] = couple_s[head] - seen[:, DK:]

    def unpacked(which, head):
        note = pair_s[which, head, 2 * DK :, :].astype(f32)
        end = note[0:1, :] + note[NOTE // 2 : NOTE // 2 + 1, :]
        return end, pair_s[which, head, 0:DK, :], pair_s[which, head, DK : 2 * DK, :]

    def compose(group):
        for r in range(ratio):
            head = group * ratio + r
            pair_copy(head).wait_recv()
            end0, map0, inject0 = unpacked(0, head)
            end1, map1, inject1 = unpacked(1, head)
            both = dot(map1, jnp.concatenate([map0, inject0], axis=1))
            transit = end1 * map0.astype(f32) + end0 * map1.astype(f32) - both[:, :DK]
            transit_s[head] = transit.astype(bf16)
            inject_s[head] = end1 * inject0.astype(f32) + inject1.astype(f32) - both[:, DK:]
            end_s[head] = jnp.broadcast_to(end1 * end0, (8, DK))

            @pl.when(has_later & jnp.logical_not(has_earlier))
            def _(head=head):
                send_s[head] = inject_s[head].astype(bf16)
                state_copy(head).start()

    def relay(group, waits):
        heads = [group * ratio + r for r in range(ratio)]

        for head in heads:
            if waits:
                state_copy(head).wait_recv()

            if waits:

                @pl.when(has_later)
                def _(head=head):
                    held = recv_s[head]
                    following = (
                        end_s[head][0:1, :] * held.astype(f32)
                        + inject_s[head]
                        - dot(transit_s[head], held)
                    )
                    send_s[head] = following.astype(bf16)
                    state_copy(head).start()

        odd = parity == 1
        for head in heads:
            held = recv_s[head]
            end0, map0, inject0 = unpacked(0, head)
            moved = end0 * held.astype(f32) + inject0.astype(f32) - dot(map0, held)
            state = jnp.where(odd, moved, held.astype(f32)).astype(bf16)
            core_out = local_s[head] + dot(couple_s[head], state)
            scale = lax.rsqrt(jnp.mean(core_out * core_out, axis=-1, keepdims=True) + EPSILON)
            columns = pl.ds(pl.multiple_of(head * DK, DK), DK)
            gate = g_ref[:, columns].astype(f32)
            hidden_s[:, columns] = (core_out * scale * gain * silu(gate)).astype(bf16)

    def slot(turn, carry):
        @pl.when(turn < key_heads)
        def _():
            local(turn)

        composing = (turn >= 1) & (turn <= key_heads)
        group = turn - 1 - stage
        relaying = (group >= 0) & (group < key_heads)

        @pl.when(composing)
        def _():
            attend(turn - 1)

        @pl.when(relaying & has_earlier)
        def _():
            relay(group, True)

        @pl.when(composing)
        def _():
            compose(turn - 1)

        @pl.when(relaying & jnp.logical_not(has_earlier))
        def _():
            relay(group, False)

        return carry

    lax.fori_loop(0, key_heads + stages, slot, 0)
    loads[10].wait()

    chunks, _, _, rows, width = part_s.shape

    def near_copy(chunk):
        return pltpu.make_async_remote_copy(
            src_ref=part_s.at[chunk, 1 - core],
            dst_ref=near_s.at[chunk],
            send_sem=near_send.at[chunk],
            recv_sem=near_recv.at[chunk],
            **at_head(twin),
        )

    def far_copy(chunk, step):
        target = lax.rem(across + step, columns_x)
        return pltpu.make_async_remote_copy(
            src_ref=sum_s.at[chunk, target],
            dst_ref=gather_s.at[chunk, step - 1],
            send_sem=far_send.at[chunk, step - 1],
            recv_sem=far_recv.at[chunk, step - 1],
            **at_head(target * 2 + core),
        )

    def project(chunk):
        product = jnp.dot(
            hidden_s[...],
            w_s[:, chunk * width : (chunk + 1) * width],
            preferred_element_type=f32,
        ).astype(bf16)
        for target in range(head_count):
            part_s[chunk, target % 2, target // 2] = product[target * rows : (target + 1) * rows]
        near_copy(chunk).start()

    def forward(chunk):
        near_copy(chunk).wait_recv()
        sum_s[chunk] = (part_s[chunk, core].astype(f32) + near_s[chunk].astype(f32)).astype(bf16)
        for step in range(1, columns_x):
            far_copy(chunk, step).start()

    lag = 2
    for turn in range(chunks + lag):
        if turn < chunks:
            project(turn)
        if turn >= lag:
            forward(turn - lag)
    for chunk in range(chunks):
        total = part_s[chunk, core, across].astype(f32) + near_s[chunk, across].astype(f32)
        for step in range(1, columns_x):
            far_copy(chunk, step).wait_recv()
            total = total + gather_s[chunk, step - 1].astype(f32)
        out_ref[:, chunk * width : (chunk + 1) * width] = total.astype(bf16)

    for chunk in range(chunks):
        near_copy(chunk).wait_send()
        for step in range(1, columns_x):
            far_copy(chunk, step).wait_send()
    for head in range(value_heads):
        pair_copy(head).wait_send()

    @pl.when(has_after)
    def _():
        for copy in rim_copies():
            copy.wait_send()

    @pl.when(has_later)
    def _():
        for head in range(value_heads):
            state_copy(head).wait_send()


def shards(seq_count, head_count, *arrays):
    query_proj, _, value_proj = arrays[:3]
    norm_gain, out_weight = arrays[9:]
    length, key_cols = query_proj.shape
    value_cols = value_proj.shape[1]
    heads = value_cols // DK
    ratio = value_cols // key_cols
    width = out_weight.shape[1]
    rows = length // head_count
    chunks = width // CHUNK
    operands = arrays[:9] + (norm_gain.reshape(1, DK), out_weight)
    columns_x = head_count // 2
    others = max(columns_x - 1, 1)
    semaphore = pltpu.SemaphoreType.DMA
    return pl.pallas_call(
        functools.partial(kernel, seq_count, head_count),
        out_shape=jax.ShapeDtypeStruct((rows, width), bf16),
        in_specs=[pl.BlockSpec(memory_space=pltpu.HBM)] * len(operands),
        out_specs=pl.BlockSpec(memory_space=pltpu.VMEM),
        scratch_shapes=[pltpu.VMEM(array.shape, array.dtype) for array in operands]
        + [
            pltpu.VMEM((RIM, key_cols), bf16),
            pltpu.VMEM((RIM, key_cols), bf16),
            pltpu.VMEM((RIM, value_cols), bf16),
            pltpu.VMEM((2 + ratio, RIM + length, DK), f32),
            pltpu.VMEM((7, HALF, HALF), bf16),
            pltpu.VMEM((heads, length, DK), f32),
            pltpu.VMEM((heads, length, DK), f32),
            pltpu.VMEM((heads, 8, length), f32),
            pltpu.VMEM((2, heads, 2 * DK + NOTE, DK), bf16),
            pltpu.VMEM((heads, DK, DK), f32),
            pltpu.VMEM((heads, DK, DK), bf16),
            pltpu.VMEM((heads, 8, DK), f32),
            pltpu.VMEM((heads, length, DK), f32),
            pltpu.VMEM((heads, length, DK), f32),
            pltpu.VMEM((heads, length, length), bf16),
            pltpu.VMEM((heads, length, 2 * DK), bf16),
            pltpu.VMEM((heads, DK, DK), bf16),
            pltpu.VMEM((heads, DK, DK), bf16),
            pltpu.VMEM((length, value_cols), bf16),
            pltpu.VMEM((chunks, 2, columns_x, rows, CHUNK), bf16),
            pltpu.VMEM((chunks, columns_x, rows, CHUNK), bf16),
            pltpu.VMEM((chunks, columns_x, rows, CHUNK), bf16),
            pltpu.VMEM((chunks, others, rows, CHUNK), bf16),
            semaphore((len(operands),)),
            semaphore((3,)),
            semaphore((3,)),
            semaphore((heads,)),
            semaphore((heads,)),
            semaphore((heads,)),
            semaphore((heads,)),
            semaphore((chunks,)),
            semaphore((chunks,)),
            semaphore((chunks, others)),
            semaphore((chunks, others)),
        ],
        compiler_params=pltpu.CompilerParams(
            collective_id=0, has_side_effects=True, vmem_limit_bytes=60 * 1024 * 1024
        ),
    )(*operands)


def solution(mesh):
    placed = (
        P("seq", "head"),
        P("seq", "head"),
        P("seq", "head"),
        P("seq", "head"),
        P("head", "seq"),
        P("head", "seq"),
        P(None, "head"),
        P(None, "head"),
        P(None, "head"),
        P(),
        P("head", None),
    )
    body = functools.partial(shards, mesh.shape["seq"], mesh.shape["head"])
    return jax.shard_map(
        body, mesh=mesh, in_specs=placed, out_specs=P(("seq", "head"), None), check_vma=False
    )
```
